768 devices in a mesh: dp: 96 (over x, z, y_lo), tensor: 8 (over y_hi, core).
Axes of the slice: x: 4, y: 8 (y_hi: 4, y_lo: 2; y = y_hi * 2 + y_lo), z: 12, core: 2. Of those that a mesh axis runs over, the one named last changes fastest.
Arguments:
- x_saved: bfloat16 [24576, 2688], P(('dp', 'tensor')), may hold values from -24 to 24
- block_scales: float32 [24576, 21], P(('dp', 'tensor')), may hold values from 0.25 to 4
- gate_grad: bfloat16 [24576, 12800], P('dp', 'tensor'), may hold values from -6 to 6
- gate_weight: bfloat16 [2688, 12800], P(None, 'tensor'), may hold values from -0.125 to 0.125
Outputs:
- input_grad: bfloat16 [24576, 2688], P(('dp', 'tensor'))
- weight_grad: float32 [2688, 12800], P('dp', 'tensor')
The draws below stay inside these ranges and needn't reach their ends.
All inputs are finite; a program needn't handle non-finite values.
Results may differ from the reference program's by a relative error of at most 0.0029.
Values may be sent and summed in bfloat16 or wider, within the bound.
A program may use at most 128 MiB of HBM per device.

```python
import math
import jax
import jax.numpy as jnp
from jax import lax

D = 2688
TOKENS = 24576
FF = 12800


def strengthened(result, stream_key, source, target, parts, factor):
    owner, partner = [(jnp.arange(result.shape[axis_at]) // (result.shape[axis_at] // parts)).reshape([-1 if axis == axis_at else 1 for axis in range(result.ndim)]) for axis_at in (source, target)]
    chosen = jax.random.permutation(stream_key, parts)[partner]
    strong = (owner == chosen) | (owner == (partner + parts // 2) % parts)
    return jnp.where(strong, factor * result, result)


def levels(rng, shape, cuts, least, high):
    loudness = 1.0
    for axis_at, blocks in cuts:
        steps = jax.random.uniform(jax.random.fold_in(jax.random.fold_in(rng, 6), axis_at), (blocks,), jnp.float32, least / len(cuts), high / len(cuts))
        loudness = loudness * jnp.repeat(jnp.exp(steps), shape[axis_at] // blocks).reshape((-1,) + (1,) * (len(shape) - 1 - axis_at))
    return loudness


def scatter_about(stream_key, shape, scale, bound, shards=(), held_as=jnp.bfloat16):
    loudness = levels(stream_key, shape, shards, -0.22, 0.18) if shards else 1.0
    values = jax.random.normal(stream_key, shape, jnp.float32) * scale * loudness
    return jnp.minimum(jnp.maximum(values, -bound), bound).astype(held_as)


def bell_draw_with(rng, shape, deviation, most, split, heavy, dtype=jnp.bfloat16):
    result = deviation * jax.random.normal(rng, shape, jnp.float32)
    if split:
        result = result * levels(rng, shape, split, -0.22, 0.18)
    return jnp.clip(strengthened(result, jax.random.fold_in(rng, 3), *heavy), -most, most).astype(dtype)


def setup_inputs(seed: int = 0) -> dict:
    streams_of = jax.random.split(jax.random.key(seed), 5)
    return {
        "x_saved": bell_draw_with(streams_of[0], (TOKENS, D), 1.0, 24.0, ((0, 768),), (0, 1, 384, 6.0)),
        "block_scales": jnp.clip(jnp.exp(math.log(4.0) - 2.7725887 * jax.random.uniform(streams_of[1], (TOKENS, D // 128), jnp.float32) ** levels(streams_of[1], (TOKENS, D // 128), ((0, 768),), -0.2, 0.2)), 0.25, 4.0),
        "gate_grad": scatter_about(streams_of[2], (TOKENS, FF), 1.0, 6.0, ((0, 96), (1, 8))),
        "gate_weight": scatter_about(streams_of[3], (D, FF), D ** -0.5, 0.125, ((1, 8),)),
    }


def reference(x_saved, block_scales, gate_grad, gate_weight):
    token_count, model_width = x_saved.shape
    block_count = block_scales.shape[1]
    scaled = x_saved.astype(jnp.float32).reshape(token_count, block_count, model_width // block_count) * block_scales[:, :, None]
    inputs = lax.optimization_barrier(scaled.reshape(token_count, model_width).astype(jnp.bfloat16))
    inputs = inputs.astype(jnp.float32)
    grad_values = gate_grad.astype(jnp.float32)
    weight_values = gate_weight.astype(jnp.float32)
    input_grad = jnp.dot(grad_values, weight_values.T, precision=lax.Precision.HIGHEST).astype(jnp.bfloat16)
    weight_sum = jnp.dot(inputs.T, grad_values, precision=lax.Precision.HIGHEST)
    weight_grad = weight_sum / math.sqrt(token_count)
    return (input_grad, weight_grad)
```

```python
import functools
import math

import jax
import jax.numpy as jnp
from jax import lax
from jax.experimental import pallas as pl
from jax.experimental.pallas import tpu as pltpu
from jax.sharding import PartitionSpec as P

MESH = pl.DeviceIdType.MESH
F32, BF16 = jnp.float32, jnp.bfloat16

NX, NZ, NL, NY, NC = 4, 12, 2, 4, 2
D, FF = 2688, 1600
ROWS = 32
GROUP = 256
DX = D // NX
DZ = DX // NZ
BLOCK = 128
PIECES = ((0, 512), (512, 512), (1024, 256), (1280, 320))
FWD, BWD = 6, 5
WCHUNK = 384


def kernel(x_ref, scale_ref, grad_ref, weight_ref, ig_ref, wg_ref, *scratch):
    (pack, a_buf, a_t, g_buf, w_buf, part, ig_part, ig_core, ig_send, ig_recv) = scratch[:10]
    n = len(PIECES)
    zf0, zb0 = scratch[10:10 + n], scratch[10 + n:10 + 2 * n]
    zf, zb = scratch[10 + 2 * n:10 + 3 * n], scratch[10 + 3 * n:10 + 4 * n]
    zl, lsend, lrecv = (scratch[10 + k * n:10 + (k + 1) * n] for k in (4, 5, 6))
    (load_sem, a2a_s, a2a_r, ya_s, ya_r, ca_s, ca_r, g_s, g_r, ic_s, ic_r, iy_s, iy_r,
     zf_s, zf_r, zb_s, zb_r, l_s, l_r) = scratch[10 + 7 * n:]

    dp, tensor = lax.axis_index("dp"), lax.axis_index("tensor")
    x, z, yl = dp // (NZ * NL), (dp // NL) % NZ, dp % NL
    yh, c = tensor // NC, tensor % NC
    s = 1 - 2 * c

    def at(x=x, z=z, yl=yl, yh=yh, c=c):
        return ((x * NZ + z) * NL + yl, yh * NC + c)

    x_to, x_from, x_opp = (x + s + NX) % NX, (x - s + NX) % NX, (x + 2) % NX
    y_to, y_from, y_opp = (yh + s + NY) % NY, (yh - s + NY) % NY, (yh + 2) % NY
    z_to, z_from = (z + s + NZ) % NZ, (z - s + NZ) % NZ
    mate = at(c=1 - c)

    pending = []

    def send(src, dst, send_sem, recv_sem, device):
        copy = pltpu.make_async_remote_copy(
            src_ref=src, dst_ref=dst, send_sem=send_sem, recv_sem=recv_sem,
            device_id=device, device_id_type=MESH,
        )
        copy.start()
        pending.append(copy)

    def arrived(dst, sem):
        pltpu.make_async_copy(dst, dst, sem).wait()

    own_grad = pltpu.make_async_copy(grad_ref, g_buf.at[x], load_sem.at[0])
    own_grad.start()
    weights = []
    for k in range(D // WCHUNK):
        rows = pl.ds(k * WCHUNK, WCHUNK)
        load = pltpu.make_async_copy(weight_ref.at[rows], w_buf.at[rows], load_sem.at[1 + k])
        load.start()
        weights.append(load)

    barrier = pltpu.get_barrier_semaphore()
    partners = [at(x=x_to), at(x=x_from), at(x=x_opp), at(yh=y_to), at(yh=y_from), at(yh=y_opp),
                at(z=z_to), at(z=z_from), at(yl=1 - yl), mate]
    for partner in partners:
        pl.semaphore_signal(barrier, inc=1, device_id=partner, device_id_type=MESH)

    scaled = jnp.concatenate(
        [x_ref[:, b * BLOCK:(b + 1) * BLOCK].astype(F32) * scale_ref[:, b:b + 1] for b in range(D // BLOCK)],
        axis=1,
    ).astype(BF16).astype(F32)
    for k in range(NX):
        pack[k] = scaled[:, k * DX:(k + 1) * DX].astype(BF16)
    pl.semaphore_wait(barrier, len(partners))

    def token_rows(yh, c):
        return pl.ds(pl.multiple_of((yh * NC + c) * ROWS, ROWS), ROWS)

    mine = token_rows(yh, c)
    for k, target in enumerate((x_to, x_from, x_opp)):
        send(pack.at[target], a_buf.at[x, mine], a2a_s.at[k], a2a_r.at[k], at(x=target))
    a_buf[x, mine] = pack[x]

    def grad_own(i):
        cols = pl.ds(*PIECES[i])
        for k, target in enumerate((x_to, x_from)):
            send(grad_ref.at[:, cols], g_buf.at[x, :, cols], g_s.at[3 * i + k], g_r.at[3 * i + k], at(x=target))

    def grad_forward(i):
        cols = pl.ds(*PIECES[i])
        block = g_buf.at[x_from, :, cols]
        arrived(block, g_r.at[3 * i])
        send(block, block, g_s.at[3 * i + 2], g_r.at[3 * i + 2], at(x=x_to))

    def grad_rest(i):
        cols = pl.ds(*PIECES[i])
        arrived(g_buf.at[x_to, :, cols], g_r.at[3 * i + 1])
        arrived(g_buf.at[x_opp, :, cols], g_r.at[3 * i + 2])

    grad_own(0)
    grad_own(1)

    for k, source in enumerate((x_from, x_to, x_opp)):
        arrived(a_buf.at[source, mine], a2a_r.at[k])
    for k, target in enumerate((y_to, y_from)):
        block = a_buf.at[:, mine]
        send(block, block, ya_s.at[k], ya_r.at[k], at(yh=target))
    send(a_buf.at[:, mine], a_buf.at[:, mine], ca_s.at[0], ca_r.at[0], mate)

    own_grad.wait()

    def ig_chunk(k):
        weights[k].wait()
        rows = pl.ds(k * WCHUNK, WCHUNK)
        prod = lax.dot_general(
            g_buf[x], w_buf[rows, :], (((1,), (1,)), ((), ())), preferred_element_type=F32
        )
        ig_part[:, :, rows] = prod.reshape(NY * NC, ROWS, WCHUNK)

    for k in range(4):
        ig_chunk(k)

    def from_y(k, source):
        block = a_buf.at[:, token_rows(source, c)]
        arrived(block, ya_r.at[k])
        send(block, block, ca_s.at[1 + k], ca_r.at[1 + k], mate)
        return block

    block = from_y(0, y_from)
    send(block, block, ya_s.at[2], ya_r.at[2], at(yh=y_to))
    grad_forward(0)
    grad_own(2)
    for k in range(4, D // WCHUNK):
        ig_chunk(k)
    for k in range(NY):
        other = (yh + k) % NY
        send(ig_part.at[other * NC + 1 - c], ig_core.at[other], ic_s.at[k], ic_r.at[k], mate)
    from_y(1, y_to)
    for k in range(NY):
        arrived(ig_core.at[(yh + k) % NY], ic_r.at[k])
    for k in range(1, NY):
        other = (yh + k) % NY
        ig_send[k - 1] = (ig_part[other * NC + c] + ig_core[other]).astype(BF16)
        send(ig_send.at[k - 1], ig_recv.at[k - 1], iy_s.at[k - 1], iy_r.at[k - 1], at(yh=other))

    grad_forward(1)
    grad_own(3)
    from_y(2, y_opp)
    for k, source in enumerate((yh, y_to, y_from, y_opp)):
        arrived(a_buf.at[:, token_rows(source, 1 - c)], ca_r.at[k])
    for k in range(NX):
        a_t[:, k * GROUP:(k + 1) * GROUP] = a_buf[k].astype(F32).T.astype(BF16)

    def multiply(i):
        start, width = PIECES[i]
        grad_rest(i)
        for first in range(0, width, 256):
            cols = pl.ds(start + first, min(256, width - first))
            rhs = jnp.concatenate([g_buf[k, :, cols] for k in range(NX)], axis=0)
            part[:, cols] = jnp.dot(a_t[...], rhs, preferred_element_type=F32)

    def own_part(i, owner):
        return part[pl.ds(pl.multiple_of(owner * DZ, 8), DZ), pl.ds(*PIECES[i])]

    def step(i, j):
        chains = (
            (FWD, z_to, (z + s * (FWD - j) + NZ) % NZ, zf0[i], zf[i], zl[i].at[0], zl[i].at[2], zf_s, zf_r),
            (BWD, z_from, (z - s * (BWD - j) + NZ) % NZ, zb0[i], zb[i], zl[i].at[1], zl[i].at[3], zb_s, zb_r),
        )
        for hops, target, owner, first, slots, last_out, last_in, ss, rs in chains:
            if j >= hops:
                continue
            value = own_part(i, owner)
            if j > 0:
                arrived(slots.at[j - 1], rs.at[i * hops + j - 1])
                value = value + slots[j - 1].astype(F32)
            if j == hops - 1:
                last_out[...] = value
                src, dst = last_out, last_in
            elif j == 0:
                first[...] = value.astype(BF16)
                src, dst = first, slots.at[0]
            else:
                slots[j - 1] = value.astype(BF16)
                src, dst = slots.at[j - 1], slots.at[j]
            send(src, dst, ss.at[i * hops + j], rs.at[i * hops + j], at(z=target))

    def close(i):
        arrived(zl[i].at[2], zf_r.at[i * FWD + FWD - 1])
        arrived(zl[i].at[3], zb_r.at[i * BWD + BWD - 1])
        lsend[i][...] = own_part(i, z) + zl[i][2] + zl[i][3]
        rows = pl.ds(pl.multiple_of((1 - yl) * 24, 8), 32)
        send(lsend[i].at[rows], lrecv[i], l_s.at[i], l_r.at[i], at(yl=1 - yl))

    def finish(i):
        arrived(lrecv[i], l_r.at[i])
        rows = pl.ds(pl.multiple_of(yl * 24, 8), 32)
        total = (lsend[i][rows, :] + lrecv[i][...]) * (1.0 / math.sqrt(GROUP * NX * NZ * NL))
        wg_ref[:, pl.ds(*PIECES[i])] = jnp.where(yl == 0, total[:28], total[4:])

    def work(i, j):
        if j < 0:
            return
        if j == 0:
            multiply(i)
        if j < FWD:
            step(i, j)
        if j == FWD:
            close(i)
        if j == FWD + 1:
            finish(i)

    def input_grad():
        total = ig_part[yh * NC + c] + ig_core[yh]
        for k in range(1, NY):
            arrived(ig_recv.at[k - 1], iy_r.at[k - 1])
            total = total + ig_recv[k - 1].astype(F32)
        ig_ref[...] = total.astype(BF16)

    offsets = (0, 1, 2, 3)
    for tick in range(FWD + 2 + offsets[-1]):
        if tick == 2:
            grad_forward(2)
        if tick == 3:
            grad_forward(3)
        if tick == 6:
            input_grad()
        for i in range(len(PIECES)):
            if tick - offsets[i] < FWD + 2:
                work(i, tick - offsets[i])
    for copy in pending:
        copy.wait_send()


def shards(x_saved, block_scales, gate_grad, gate_weight):
    widths = [w for _, w in PIECES]
    dma = pltpu.SemaphoreType.DMA
    vmem, hbm = pl.BlockSpec(memory_space=pltpu.VMEM), pl.BlockSpec(memory_space=pl.ANY)
    n = len(PIECES)
    return pl.pallas_call(
        kernel,
        out_shape=(jax.ShapeDtypeStruct((ROWS, D), BF16), jax.ShapeDtypeStruct((28, FF), F32)),
        in_specs=[vmem, vmem, hbm, hbm],
        out_specs=(vmem, vmem),
        scratch_shapes=[
            pltpu.VMEM((NX, ROWS, DX), BF16),
            pltpu.VMEM((NX, GROUP, DX), BF16),
            pltpu.VMEM((DX, NX * GROUP), BF16),
            pltpu.VMEM((NX, GROUP, FF), BF16),
            pltpu.VMEM((D, FF), BF16),
            pltpu.VMEM((DX, FF), F32),
            pltpu.VMEM((NY * NC, ROWS, D), F32),
            pltpu.VMEM((NY, ROWS, D), F32),
            pltpu.VMEM((NY - 1, ROWS, D), BF16),
            pltpu.VMEM((NY - 1, ROWS, D), BF16),
            *[pltpu.VMEM((DZ, w), BF16) for w in widths],
            *[pltpu.VMEM((DZ, w), BF16) for w in widths],
            *[pltpu.VMEM((FWD - 1, DZ, w), BF16) for w in widths],
            *[pltpu.VMEM((BWD - 1, DZ, w), BF16) for w in widths],
            *[pltpu.VMEM((4, DZ, w), F32) for w in widths],
            *[pltpu.VMEM((DZ, w), F32) for w in widths],
            *[pltpu.VMEM((32, w), F32) for w in widths],
            dma((1 + D // WCHUNK,)),
            dma((3,)), dma((3,)), dma((3,)), dma((3,)), dma((4,)), dma((4,)),
            dma((3 * n,)), dma((3 * n,)), dma((4,)), dma((4,)), dma((3,)), dma((3,)),
            dma((FWD * n,)), dma((FWD * n,)), dma((BWD * n,)), dma((BWD * n,)), dma((n,)), dma((n,)),
        ],
        compiler_params=pltpu.CompilerParams(
            collective_id=0, has_side_effects=True, vmem_limit_bytes=56 * 2**20
        ),
        cost_estimate=pl.CostEstimate(flops=4 * GROUP * D * FF, bytes_accessed=12 * 2**20, transcendentals=0),
    )(x_saved, block_scales, gate_grad, gate_weight)


def solution(mesh):
    return jax.shard_map(
        shards,
        mesh=mesh,
        in_specs=(
            P(("dp", "tensor"), None),
            P(("dp", "tensor"), None),
            P("dp", "tensor"),
            P(None, "tensor"),
        ),
        out_specs=(P(("dp", "tensor"), None), P("dp", "tensor")),
        check_vma=False,
    )
```

```python
import math

import jax
import jax.numpy as jnp
from jax import lax
from jax.experimental import pallas as pl
from jax.experimental.pallas import tpu as pltpu
from jax.sharding import PartitionSpec as P

MESH = pl.DeviceIdType.MESH
F32, BF16 = jnp.float32, jnp.bfloat16

NX, NZ, NL, NY, NC = 4, 12, 2, 4, 2
D, FF = 2688, 1600
ROWS, GROUP = 32, 256
DX, DL = D // NX, D // (NX * NZ * NL)
BLOCK = 128
PER = (16, 12)
HALF = tuple(NL * p for p in PER)
WIDTH = tuple(NZ * h for h in HALF)
UNITS = ((0, 256), (256, 256), (512, 256), (768, 256), (1024, 256), (1280, 320))
JOBS = (
    ((0,), (0,), True),
    ((0,), (1,), True),
    ((1,), (0, 1), True),
    ((0, 1), (2,), True),
    ((0, 1), (3,), True),
    ((0, 1), (4,), False),
    ((0, 1), (5,), False),
)
ORDER = (
    "pack0", "scatter0", "own0", "pack1", "scatter1", "own1", "ig0", "ig1", "ig2", "ig3", "fwd0", "ig4", "ig5",
    "rest0", "ig6", "igmate", "fwd1", "rest1", "mate01", "mate03", "fwd2", "mate11", "mate13", "fwd3", "mate02",
    "st00", "st10", "mate12", "igo1", "igo2", "igo3", "st20", "st01", "st11", "fwd4", "st30", "st21", "st02", "st12",
    "st40", "st31", "fwd5", "st22", "st03", "st13", "st41", "st32", "st50", "st23", "st04", "st14", "st60", "st42",
    "st33", "st51", "st24", "st05", "st15", "st61", "st43", "igfin", "st34", "st25", "st52", "close0", "close1",
    "st62", "st35", "st44", "fin0", "close2", "fin1", "st53", "st63", "close3", "st45", "fin2", "st54", "st64",
    "fin3", "close4", "st55", "st65", "fin4", "close5", "close6", "fin5", "fin6",
)
FWD, BWD = 6, 5
WCHUNK = 384


def job_rows(job):
    return sum(HALF[h] for h in job[0])


def job_cols(job):
    first, last = UNITS[job[1][0]], UNITS[job[1][-1]]
    return first[0], last[0] + last[1] - first[0]


def kernel(x_ref, scale_ref, grad_ref, weight_ref, ig_ref, wg_ref, *scratch):
    scratch = list(scratch)

    def take(count=None):
        if count is None:
            return scratch.pop(0)
        return [scratch.pop(0) for _ in range(count)]

    n, h2 = len(JOBS), len(HALF)
    pack, a_buf = take(h2), take(h2)
    g_buf, w_buf, part, ig_part, ig_core, ig_send, ig_recv = take(7)
    first_out, slots, last_out, last_in, total_buf, low_out, low_in = (take(n) for _ in range(7))
    (load_sem, a2a_s, a2a_r, ya_s, ya_r, ca_s, ca_r, g_s, g_r, ic_s, ic_r, iy_s, iy_r,
     z_s, z_r, l_s, l_r) = scratch

    dp, tensor = lax.axis_index("dp"), lax.axis_index("tensor")
    x, z, yl = dp // (NZ * NL), (dp // NL) % NZ, dp % NL
    yh, c = tensor // NC, tensor % NC
    s = 1 - 2 * c

    def at(x=x, z=z, yl=yl, yh=yh, c=c):
        return ((x * NZ + z) * NL + yl, yh * NC + c)

    x_to, x_from = (x + s + NX) % NX, (x - s + NX) % NX
    z_to, z_from = (z + s + NZ) % NZ, (z - s + NZ) % NZ
    y_to, y_from, y_opp = (yh + s + NY) % NY, (yh - s + NY) % NY, (yh + 2) % NY
    slot_to, slot_from = (NX + s) % NX, (NX - s) % NX
    mate = at(c=1 - c)
    x_other = [(x + k) % NX for k in range(NX)]
    y_other = [(yh + k) % NY for k in range(NY)]

    pending = []

    def send(src, dst, send_sem, recv_sem, device):
        copy = pltpu.make_async_remote_copy(
            src_ref=src, dst_ref=dst, send_sem=send_sem, recv_sem=recv_sem,
            device_id=device, device_id_type=MESH,
        )
        copy.start()
        pending.append(copy)

    def arrived(dst, sem):
        pltpu.make_async_copy(dst, dst, sem).wait()

    barrier = pltpu.get_barrier_semaphore()
    partners = [at(x=o) for o in x_other[1:]] + [at(yh=o) for o in y_other[1:]] + [
        at(z=z_to), at(z=z_from), at(yl=1 - yl), mate]
    for partner in partners:
        pl.semaphore_signal(barrier, inc=1, device_id=partner, device_id_type=MESH)

    own_grad = pltpu.make_async_copy(grad_ref, g_buf.at[0], load_sem.at[0])
    own_grad.start()
    weights = []
    for k in range(D // WCHUNK):
        cols = pl.ds(k * WCHUNK, WCHUNK)
        load = pltpu.make_async_copy(weight_ref.at[:, cols], w_buf.at[:, cols], load_sem.at[1 + k])
        load.start()
        weights.append(load)

    scale = scale_ref[...].T
    scaled = jnp.concatenate(
        [(x_ref[:, b * BLOCK:(b + 1) * BLOCK].astype(F32) * scale[:, b:b + 1]).astype(BF16)
         for b in range(D // BLOCK)],
        axis=1,
    ).astype(F32)

    def token_rows(yh, c):
        return pl.ds(pl.multiple_of((yh * NC + c) * ROWS, ROWS), ROWS)

    mine = token_rows(yh, c)

    def pack_half(h):
        for k in range(NX):
            pack[h][k] = jnp.concatenate(
                [scaled[:, k * DX + DL * j + sum(PER[:h]):k * DX + DL * j + sum(PER[:h + 1])]
                 for j in range(NZ * NL)],
                axis=1,
            ).astype(BF16)

    def scatter_half(h):
        for k in range(1, NX):
            index = 3 * h + k - 1
            send(pack[h].at[x_other[k]], a_buf[h].at[NX - k, mine], a2a_s.at[index], a2a_r.at[index],
                 at(x=x_other[k]))
        a_buf[h][0, mine] = pack[h][x]
        share(h, 0)

    def columns(p):
        return pl.ds(0, 1) if p == 0 else pl.ds(1, NX - 1)

    def share(h, p):
        block = a_buf[h].at[columns(p), mine]
        for k, target in enumerate((y_to, y_from)):
            index = h * 5 + k * 2 + p
            send(block, block, ya_s.at[index], ya_r.at[index], at(yh=target))
        send(block, block, ca_s.at[h * 2 + p], ca_r.at[h * 2 + p], mate)

    def share_rest(h):
        for k in range(1, NX):
            index = 3 * h + k - 1
            arrived(a_buf[h].at[NX - k, mine], a2a_r.at[index])
        share(h, 1)

    def to_mate(h, k):
        block = a_buf[h].at[:, token_rows((y_from, y_opp, y_to)[k - 1], c)]
        if k == 2:
            arrived(block, ya_r.at[h * 5 + 4])
        else:
            for p in (0, 1):
                part_ = a_buf[h].at[columns(p), token_rows(y_from if k == 1 else y_to, c)]
                arrived(part_, ya_r.at[h * 5 + (k // 2) * 2 + p])
        if k == 1:
            send(block, block, ya_s.at[h * 5 + 4], ya_r.at[h * 5 + 4], at(yh=y_to))
        index = 4 + h * 3 + k - 1
        send(block, block, ca_s.at[index], ca_r.at[index], mate)

    def inputs_ready(h):
        for p in (0, 1):
            arrived(a_buf[h].at[columns(p), token_rows(yh, 1 - c)], ca_r.at[h * 2 + p])
        for k, source in enumerate((y_to, y_opp, y_from)):
            arrived(a_buf[h].at[:, token_rows(source, 1 - c)], ca_r.at[4 + h * 3 + k])

    def grad_own(i):
        units = pl.ds(*UNITS[i])
        for k, (target, slot) in enumerate(((x_to, slot_from), (x_from, slot_to))):
            send(grad_ref.at[units], g_buf.at[slot, units], g_s.at[3 * i + k], g_r.at[3 * i + k], at(x=target))

    def grad_forward(i):
        units = pl.ds(*UNITS[i])
        arrived(g_buf.at[slot_from, units], g_r.at[3 * i])
        send(g_buf.at[slot_from, units], g_buf.at[2, units], g_s.at[3 * i + 2], g_r.at[3 * i + 2], at(x=x_to))

    def grad_ready(i):
        units = pl.ds(*UNITS[i])
        arrived(g_buf.at[slot_to, units], g_r.at[3 * i + 1])
        arrived(g_buf.at[2, units], g_r.at[3 * i + 2])

    def ig_chunk(k):
        if k == 0:
            own_grad.wait()
        weights[k].wait()
        cols = pl.ds(k * WCHUNK, WCHUNK)
        prod = lax.dot_general(
            g_buf[0], w_buf[:, cols], (((0,), (0,)), ((), ())), preferred_element_type=F32
        )
        ig_part[:, :, cols] = prod.reshape(NY * NC, ROWS, WCHUNK)

    def ig_to_mate():
        for k in range(NY):
            other = y_other[k]
            send(ig_part.at[other * NC + 1 - c], ig_core.at[other], ic_s.at[k], ic_r.at[k], mate)

    def ig_to_owner(k):
        other = y_other[k]
        arrived(ig_core.at[other], ic_r.at[k])
        ig_send[k - 1] = (ig_part[other * NC + c] + ig_core[other]).astype(BF16)
        send(ig_send.at[k - 1], ig_recv.at[k - 1], iy_s.at[k - 1], iy_r.at[k - 1], at(yh=other))

    def ig_finish():
        arrived(ig_core.at[yh], ic_r.at[0])
        total = ig_part[yh * NC + c] + ig_core[yh]
        for k in range(1, NY):
            arrived(ig_recv.at[k - 1], iy_r.at[k - 1])
            total = total + ig_recv[k - 1].astype(F32)
        ig_ref[...] = total.astype(BF16)

    half_seen, unit_seen = set(), set()

    def multiply(i):
        halves, units, _ = JOBS[i]
        for u in units:
            if u not in unit_seen:
                unit_seen.add(u)
                grad_ready(u)
        for h in halves:
            if h not in half_seen:
                half_seen.add(h)
                inputs_ready(h)
        cols = pl.ds(*job_cols(JOBS[i]))
        for h in halves:
            total = None
            for k in range(NX):
                prod = lax.dot_general(
                    a_buf[h][k], g_buf[k, cols], (((0,), (1,)), ((), ())), preferred_element_type=F32
                )
                total = prod if k == 0 else total + prod
            part[sum(WIDTH[:h]):sum(WIDTH[:h + 1]), cols] = total

    def own_part(i, owner):
        cols = pl.ds(*job_cols(JOBS[i]))
        blocks = [
            part[pl.ds(pl.multiple_of(sum(WIDTH[:h]) + owner * HALF[h], 8), HALF[h]), cols] for h in JOBS[i][0]
        ]
        return blocks[0] if len(blocks) == 1 else jnp.concatenate(blocks, axis=0)

    def step(i, j):
        if j == 0:
            multiply(i)
        for d, (hops, target, sign) in enumerate(((FWD, z_to, s), (BWD, z_from, -s))):
            if j >= hops:
                continue
            base, sem = d * (FWD - 1), i * (FWD + BWD) + d * FWD
            value = own_part(i, (z + sign * (hops - j) + NZ) % NZ)
            if j > 0:
                arrived(slots[i].at[base + j - 1], z_r.at[sem + j - 1])
                value = value + slots[i][base + j - 1].astype(F32)
            if j == hops - 1:
                last_out[i][d] = value.astype(last_out[i].dtype)
                src, dst = last_out[i].at[d], last_in[i].at[d]
            elif j == 0:
                first_out[i][d] = value.astype(BF16)
                src, dst = first_out[i].at[d], slots[i].at[base]
            else:
                slots[i][base + j - 1] = value.astype(BF16)
                src, dst = slots[i].at[base + j - 1], slots[i].at[base + j]
            send(src, dst, z_s.at[sem + j], z_r.at[sem + j], at(z=target))

    def low_blocks(i, low):
        base, blocks = 0, []
        for h in JOBS[i][0]:
            blocks.append(total_buf[i][pl.ds(pl.multiple_of(base + low * (8 * (h == 1) + 16 * (h == 0)), 8), 16), :])
            base += HALF[h]
        return blocks

    def close(i):
        arrived(last_in[i].at[0], z_r.at[i * (FWD + BWD) + FWD - 1])
        arrived(last_in[i].at[1], z_r.at[i * (FWD + BWD) + FWD + BWD - 1])
        total_buf[i][...] = own_part(i, z) + last_in[i][0].astype(F32) + last_in[i][1].astype(F32)
        for k, block in enumerate(low_blocks(i, 1 - yl)):
            low_out[i][16 * k:16 * k + 16, :] = block
        send(low_out[i], low_in[i], l_s.at[i], l_r.at[i], at(yl=1 - yl))

    def finish(i):
        arrived(low_in[i], l_r.at[i])
        cols = pl.ds(*job_cols(JOBS[i]))
        for k, (h, block) in enumerate(zip(JOBS[i][0], low_blocks(i, yl))):
            total = (block + low_in[i][16 * k:16 * k + 16, :]) * (1.0 / math.sqrt(GROUP * NX * NZ * NL))
            if h == 0:
                wg_ref[0:16, cols] = total
            else:
                wg_ref[16:28, cols] = jnp.where(yl == 0, total[:12], total[4:])

    def enter(h):
        if h == 0:
            pl.semaphore_wait(barrier, len(partners))
        scatter_half(h)

    def forward(i):
        grad_forward(i)
        if i + 2 < len(UNITS):
            grad_own(i + 2)

    what = dict(pack=pack_half, scatter=enter, own=grad_own, rest=share_rest, fwd=forward, mate=to_mate, ig=ig_chunk,
                igmate=ig_to_mate, igo=ig_to_owner, igfin=ig_finish, st=step, close=close, fin=finish)
    for name in ORDER:
        word = name.rstrip("0123456789")
        what[word](*(int(digit) for digit in name[len(word):]))
    for copy in pending:
        copy.wait_send()


def shards(x_saved, block_scales, gate_grad, gate_weight):
    dma = pltpu.SemaphoreType.DMA
    vmem, hbm = pl.BlockSpec(memory_space=pltpu.VMEM), pl.BlockSpec(memory_space=pl.ANY)
    n, u, hops = len(JOBS), len(UNITS), FWD + BWD
    shapes = [(job_rows(job), job_cols(job)[1]) for job in JOBS]
    lasts = [F32 if job[2] else BF16 for job in JOBS]
    return pl.pallas_call(
        kernel,
        out_shape=(jax.ShapeDtypeStruct((ROWS, D), BF16), jax.ShapeDtypeStruct((DL, FF), F32)),
        in_specs=[vmem, vmem, hbm, hbm],
        out_specs=(vmem, vmem),
        scratch_shapes=[
            *[pltpu.VMEM((NX, ROWS, w), BF16) for w in WIDTH],
            *[pltpu.VMEM((NX, GROUP, w), BF16) for w in WIDTH],
            pltpu.VMEM((NX, FF, GROUP), BF16),
            pltpu.VMEM((FF, D), BF16),
            pltpu.VMEM((DX, FF), F32),
            pltpu.VMEM((NY * NC, ROWS, D), F32),
            pltpu.VMEM((NY, ROWS, D), F32),
            pltpu.VMEM((NY - 1, ROWS, D), BF16),
            pltpu.VMEM((NY - 1, ROWS, D), BF16),
            *[pltpu.VMEM((2, *shape), BF16) for shape in shapes],
            *[pltpu.VMEM((hops - 2, *shape), BF16) for shape in shapes],
            *[pltpu.VMEM((2, *shape), last) for shape, last in zip(shapes, lasts)],
            *[pltpu.VMEM((2, *shape), last) for shape, last in zip(shapes, lasts)],
            *[pltpu.VMEM(shape, F32) for shape in shapes],
            *[pltpu.VMEM((16 * len(job[0]), shape[1]), F32) for job, shape in zip(JOBS, shapes)],
            *[pltpu.VMEM((16 * len(job[0]), shape[1]), F32) for job, shape in zip(JOBS, shapes)],
            dma((1 + D // WCHUNK,)),
            dma((6,)), dma((6,)), dma((10,)), dma((10,)), dma((10,)), dma((10,)),
            dma((3 * u,)), dma((3 * u,)), dma((4,)), dma((4,)), dma((3,)), dma((3,)),
            dma((hops * n,)), dma((hops * n,)), dma((n,)), dma((n,)),
        ],
        compiler_params=pltpu.CompilerParams(
            collective_id=0, has_side_effects=True, vmem_limit_bytes=56 * 2**20
        ),
        cost_estimate=pl.CostEstimate(flops=4 * GROUP * D * FF, bytes_accessed=12 * 2**20, transcendentals=0),
    )(x_saved, block_scales.T, gate_grad.T, gate_weight.T)


def solution(mesh):
    return jax.shard_map(
        shards,
        mesh=mesh,
        in_specs=(
            P(("dp", "tensor"), None),
            P(("dp", "tensor"), None),
            P("dp", "tensor"),
            P(None, "tensor"),
        ),
        out_specs=(P(("dp", "tensor"), None), P("dp", "tensor")),
        check_vma=False,
    )
```

```python
import math

import jax
import jax.numpy as jnp
from jax import lax
from jax.experimental import pallas as pl
from jax.experimental.pallas import tpu as pltpu
from jax.sharding import PartitionSpec as P

MESH = pl.DeviceIdType.MESH
F32, BF16 = jnp.float32, jnp.bfloat16

NX, NZ, NL, NY, NC = 4, 12, 2, 4, 2
D, FF = 2688, 1600
ROWS, GROUP = 32, 256
DX, DL = D // NX, D // (NX * NZ * NL)
BLOCK = 128
PER = (16, 12)
HALF = tuple(NL * p for p in PER)
WIDTH = tuple(NZ * h for h in HALF)
UNITS = ((0, 256), (256, 256), (512, 256), (768, 256), (1024, 256), (1280, 320))
JOBS = (
    ((0,), (0,), True),
    ((0,), (1,), True),
    ((1,), (0, 1), True),
    ((0, 1), (2,), True),
    ((0, 1), (3,), True),
    ((0, 1), (4,), False),
    ((0, 1), (5,), False),
)
DUAL = (5, 6)
ORDER = (
    "pack0", "scatter0", "own0", "pack1", "scatter1", "own1", "ig0", "ig1", "ig2", "ig3", "fwd0", "ig4", "ig5",
    "rest0", "ig6", "igmate", "fwd1", "rest1", "mate01", "mate03", "fwd2", "mate11", "mate13", "fwd3", "mate02",
    "st00", "st10", "mate12", "igo1", "igo2", "igo3", "st20", "st01", "st11", "fwd4", "st30", "st21", "st02", "st12",
    "st40", "st31", "fwd5", "st22", "st03", "st13", "st41", "st32", "st50", "st04", "st14", "st23", "st60", "st42",
    "st33", "st51", "st05", "st15", "st24", "st61", "igfin", "st43", "st34", "close0", "close1", "st52", "st25",
    "st62", "st35", "fin0", "st44", "fin1", "close2", "st53", "st63", "close3", "st45", "fin2", "st54", "st64",
    "fin3", "close4", "st55", "st65", "fin4", "fin5", "fin6",
)
FWD, BWD = 6, 5
WCHUNK = 384


def job_rows(job):
    return sum(HALF[h] for h in job[0])


def job_cols(job):
    first, last = UNITS[job[1][0]], UNITS[job[1][-1]]
    return first[0], last[0] + last[1] - first[0]


def kernel(x_ref, scale_ref, grad_ref, weight_ref, ig_ref, wg_ref, *scratch):
    scratch = list(scratch)

    def take(count=None):
        if count is None:
            return scratch.pop(0)
        return [scratch.pop(0) for _ in range(count)]

    n, h2 = len(JOBS), len(HALF)
    pack, a_buf = take(h2), take(h2)
    x_buf, scale_buf, g_buf, w_buf, part, ig_part, ig_core, ig_send, ig_recv = take(9)
    first_out, slots, last_out, last_in, total_buf, low_out, low_in = (take(n) for _ in range(7))
    value_buf = dict(zip(DUAL, take(len(DUAL))))
    (load_sem, a2a_s, a2a_r, ya_s, ya_r, ca_s, ca_r, g_s, g_r, ic_s, ic_r, iy_s, iy_r,
     z_s, z_r, l_s, l_r, o_s, o_r) = scratch

    dp, tensor = lax.axis_index("dp"), lax.axis_index("tensor")
    x, z, yl = dp // (NZ * NL), (dp // NL) % NZ, dp % NL
    yh, c = tensor // NC, tensor % NC
    s = 1 - 2 * c

    def at(x=x, z=z, yl=yl, yh=yh, c=c):
        return ((x * NZ + z) * NL + yl, yh * NC + c)

    x_to, x_from = (x + s + NX) % NX, (x - s + NX) % NX
    z_to, z_from = (z + s + NZ) % NZ, (z - s + NZ) % NZ
    y_to, y_from, y_opp = (yh + s + NY) % NY, (yh - s + NY) % NY, (yh + 2) % NY
    slot_to, slot_from = (NX + s) % NX, (NX - s) % NX
    mate = at(c=1 - c)
    x_other = [(x + k) % NX for k in range(NX)]
    y_other = [(yh + k) % NY for k in range(NY)]

    pending = []

    def send(src, dst, send_sem, recv_sem, device):
        copy = pltpu.make_async_remote_copy(
            src_ref=src, dst_ref=dst, send_sem=send_sem, recv_sem=recv_sem,
            device_id=device, device_id_type=MESH,
        )
        copy.start()
        pending.append(copy)

    def arrived(dst, sem):
        pltpu.make_async_copy(dst, dst, sem).wait()

    loads = []
    for k, (src, dst) in enumerate(((x_ref, x_buf), (scale_ref, scale_buf))):
        load = pltpu.make_async_copy(src, dst, load_sem.at[1 + D // WCHUNK + k])
        load.start()
        loads.append(load)

    barrier = pltpu.get_barrier_semaphore()
    partners = [at(x=o) for o in x_other[1:]] + [at(yh=o) for o in y_other[1:]] + [
        at(z=z_to), at(z=z_from), at(z=z_to, yl=1 - yl), at(z=z_from, yl=1 - yl), at(yl=1 - yl), mate]
    for partner in partners:
        pl.semaphore_signal(barrier, inc=1, device_id=partner, device_id_type=MESH)

    own_grad = pltpu.make_async_copy(grad_ref, g_buf.at[0], load_sem.at[0])
    own_grad.start()
    weights = []
    for k in range(D // WCHUNK):
        cols = pl.ds(k * WCHUNK, WCHUNK)
        load = pltpu.make_async_copy(weight_ref.at[:, cols], w_buf.at[:, cols], load_sem.at[1 + k])
        load.start()
        weights.append(load)

    for load in loads:
        load.wait()
    scale = scale_buf[...].T
    scaled = jnp.concatenate(
        [(x_buf[:, b * BLOCK:(b + 1) * BLOCK].astype(F32) * scale[:, b:b + 1]).astype(BF16)
         for b in range(D // BLOCK)],
        axis=1,
    ).astype(F32)

    def token_rows(yh, c):
        return pl.ds(pl.multiple_of((yh * NC + c) * ROWS, ROWS), ROWS)

    mine = token_rows(yh, c)

    def pack_half(h):
        for k in range(NX):
            pack[h][k] = jnp.concatenate(
                [scaled[:, k * DX + DL * j + sum(PER[:h]):k * DX + DL * j + sum(PER[:h + 1])]
                 for j in range(NZ * NL)],
                axis=1,
            ).astype(BF16)

    def scatter_half(h):
        for k in range(1, NX):
            index = 3 * h + k - 1
            send(pack[h].at[x_other[k]], a_buf[h].at[NX - k, mine], a2a_s.at[index], a2a_r.at[index],
                 at(x=x_other[k]))
        a_buf[h][0, mine] = pack[h][x]
        share(h, 0)

    def columns(p):
        return pl.ds(0, 1) if p == 0 else pl.ds(1, NX - 1)

    def share(h, p):
        block = a_buf[h].at[columns(p), mine]
        for k, target in enumerate((y_to, y_from)):
            index = h * 5 + k * 2 + p
            send(block, block, ya_s.at[index], ya_r.at[index], at(yh=target))
        send(block, block, ca_s.at[h * 2 + p], ca_r.at[h * 2 + p], mate)

    def share_rest(h):
        for k in range(1, NX):
            index = 3 * h + k - 1
            arrived(a_buf[h].at[NX - k, mine], a2a_r.at[index])
        share(h, 1)

    def to_mate(h, k):
        block = a_buf[h].at[:, token_rows((y_from, y_opp, y_to)[k - 1], c)]
        if k == 2:
            arrived(block, ya_r.at[h * 5 + 4])
        else:
            for p in (0, 1):
                part_ = a_buf[h].at[columns(p), token_rows(y_from if k == 1 else y_to, c)]
                arrived(part_, ya_r.at[h * 5 + (k // 2) * 2 + p])
        if k == 1:
            send(block, block, ya_s.at[h * 5 + 4], ya_r.at[h * 5 + 4], at(yh=y_to))
        index = 4 + h * 3 + k - 1
        send(block, block, ca_s.at[index], ca_r.at[index], mate)

    def inputs_ready(h):
        for p in (0, 1):
            arrived(a_buf[h].at[columns(p), token_rows(yh, 1 - c)], ca_r.at[h * 2 + p])
        for k, source in enumerate((y_to, y_opp, y_from)):
            arrived(a_buf[h].at[:, token_rows(source, 1 - c)], ca_r.at[4 + h * 3 + k])

    def grad_own(i):
        units = pl.ds(*UNITS[i])
        for k, (target, slot) in enumerate(((x_to, slot_from), (x_from, slot_to))):
            send(grad_ref.at[units], g_buf.at[slot, units], g_s.at[3 * i + k], g_r.at[3 * i + k], at(x=target))

    def grad_forward(i):
        units = pl.ds(*UNITS[i])
        arrived(g_buf.at[slot_from, units], g_r.at[3 * i])
        send(g_buf.at[slot_from, units], g_buf.at[2, units], g_s.at[3 * i + 2], g_r.at[3 * i + 2], at(x=x_to))

    def grad_ready(i):
        units = pl.ds(*UNITS[i])
        arrived(g_buf.at[slot_to, units], g_r.at[3 * i + 1])
        arrived(g_buf.at[2, units], g_r.at[3 * i + 2])

    def ig_chunk(k):
        if k == 0:
            own_grad.wait()
        weights[k].wait()
        cols = pl.ds(k * WCHUNK, WCHUNK)
        prod = lax.dot_general(
            g_buf[0], w_buf[:, cols], (((0,), (0,)), ((), ())), preferred_element_type=F32
        )
        ig_part[:, :, cols] = prod.reshape(NY * NC, ROWS, WCHUNK)

    def ig_to_mate():
        for k in range(NY):
            other = y_other[k]
            send(ig_part.at[other * NC + 1 - c], ig_core.at[other], ic_s.at[k], ic_r.at[k], mate)

    def ig_to_owner(k):
        other = y_other[k]
        arrived(ig_core.at[other], ic_r.at[k])
        ig_send[k - 1] = (ig_part[other * NC + c] + ig_core[other]).astype(BF16)
        send(ig_send.at[k - 1], ig_recv.at[k - 1], iy_s.at[k - 1], iy_r.at[k - 1], at(yh=other))

    def ig_finish():
        arrived(ig_core.at[yh], ic_r.at[0])
        total = ig_part[yh * NC + c] + ig_core[yh]
        for k in range(1, NY):
            arrived(ig_recv.at[k - 1], iy_r.at[k - 1])
            total = total + ig_recv[k - 1].astype(F32)
        ig_ref[...] = total.astype(BF16)

    half_seen, unit_seen = set(), set()

    def multiply(i):
        halves, units, _ = JOBS[i]
        for u in units:
            if u not in unit_seen:
                unit_seen.add(u)
                grad_ready(u)
        for h in halves:
            if h not in half_seen:
                half_seen.add(h)
                inputs_ready(h)
        cols = pl.ds(*job_cols(JOBS[i]))
        for h in halves:
            total = None
            for k in range(NX):
                prod = lax.dot_general(
                    a_buf[h][k], g_buf[k, cols], (((0,), (1,)), ((), ())), preferred_element_type=F32
                )
                total = prod if k == 0 else total + prod
            part[sum(WIDTH[:h]):sum(WIDTH[:h + 1]), cols] = total

    def own_part(i, owner):
        cols = pl.ds(*job_cols(JOBS[i]))
        blocks = [
            part[pl.ds(pl.multiple_of(sum(WIDTH[:h]) + owner * HALF[h], 8), HALF[h]), cols] for h in JOBS[i][0]
        ]
        return blocks[0] if len(blocks) == 1 else jnp.concatenate(blocks, axis=0)

    def step(i, j):
        if j == 0:
            multiply(i)
            if i in DUAL:
                total_buf[i][...] = own_part(i, z)
                low_send(i)
        for d, (hops, target, sign) in enumerate(((FWD, z_to, s), (BWD, z_from, -s))):
            if j >= hops:
                continue
            base, sem = d * (FWD - 1), i * (FWD + BWD) + d * FWD
            value = own_part(i, (z + sign * (hops - j) + NZ) % NZ)
            if j > 0:
                arrived(slots[i].at[base + j - 1], z_r.at[sem + j - 1])
                value = value + slots[i][base + j - 1].astype(F32)
            if j == hops - 1 and i in DUAL:
                last_both(i, d, value, target, sem + j)
                continue
            if j == hops - 1:
                last_out[i][d] = value.astype(last_out[i].dtype)
                src, dst = last_out[i].at[d], last_in[i].at[d]
            elif j == 0:
                first_out[i][d] = value.astype(BF16)
                src, dst = first_out[i].at[d], slots[i].at[base]
            else:
                slots[i][base + j - 1] = value.astype(BF16)
                src, dst = slots[i].at[base + j - 1], slots[i].at[base + j]
            send(src, dst, z_s.at[sem + j], z_r.at[sem + j], at(z=target))

    def low_blocks(i, ref, low):
        base, blocks = 0, []
        for h in JOBS[i][0]:
            blocks.append(ref[pl.ds(pl.multiple_of(base + low * (8 * (h == 1) + 16 * (h == 0)), 8), 16), :])
            base += HALF[h]
        return blocks

    def low_send(i):
        for k, block in enumerate(low_blocks(i, total_buf[i], 1 - yl)):
            low_out[i][16 * k:16 * k + 16, :] = block
        send(low_out[i], low_in[i], l_s.at[i], l_r.at[i], at(yl=1 - yl))

    def last_both(i, d, value, target, sem):
        scratch_ = value_buf[i].at[d]
        scratch_[...] = value
        for q, low in enumerate((yl, 1 - yl)):
            for k, block in enumerate(low_blocks(i, scratch_, low)):
                last_out[i][d, q, 16 * k:16 * k + 16, :] = block.astype(BF16)
            index = 2 * DUAL.index(i) + d
            ss, rs = (z_s.at[sem], z_r.at[sem]) if q == 0 else (o_s.at[index], o_r.at[index])
            send(last_out[i].at[d, q], last_in[i].at[d, q], ss, rs, at(z=target, yl=low))

    def close(i):
        arrived(last_in[i].at[0], z_r.at[i * (FWD + BWD) + FWD - 1])
        arrived(last_in[i].at[1], z_r.at[i * (FWD + BWD) + FWD + BWD - 1])
        total_buf[i][...] = own_part(i, z) + last_in[i][0].astype(F32) + last_in[i][1].astype(F32)
        low_send(i)

    def finish(i):
        arrived(low_in[i], l_r.at[i])
        extra = None
        if i in DUAL:
            for d, hops in enumerate((FWD, BWD)):
                arrived(last_in[i].at[d, 0], z_r.at[i * (FWD + BWD) + d * FWD + hops - 1])
                arrived(last_in[i].at[d, 1], o_r.at[2 * DUAL.index(i) + d])
            extra = sum(last_in[i][d, q].astype(F32) for d in (0, 1) for q in (0, 1))
        cols = pl.ds(*job_cols(JOBS[i]))
        for k, (h, block) in enumerate(zip(JOBS[i][0], low_blocks(i, total_buf[i], yl))):
            total = block + low_in[i][16 * k:16 * k + 16, :]
            if extra is not None:
                total = total + extra[16 * k:16 * k + 16]
            total = total * (1.0 / math.sqrt(GROUP * NX * NZ * NL))
            if h == 0:
                wg_ref[0:16, cols] = total
            else:
                wg_ref[16:28, cols] = jnp.where(yl == 0, total[:12], total[4:])

    def enter(h):
        if h == 0:
            pl.semaphore_wait(barrier, len(partners))
        scatter_half(h)

    def forward(i):
        grad_forward(i)
        if i + 2 < len(UNITS):
            grad_own(i + 2)

    what = dict(pack=pack_half, scatter=enter, own=grad_own, rest=share_rest, fwd=forward, mate=to_mate, ig=ig_chunk,
                igmate=ig_to_mate, igo=ig_to_owner, igfin=ig_finish, st=step, close=close, fin=finish)
    for name in ORDER:
        word = name.rstrip("0123456789")
        what[word](*(int(digit) for digit in name[len(word):]))
    for copy in pending:
        copy.wait_send()


def shards(x_saved, block_scales, gate_grad, gate_weight):
    dma = pltpu.SemaphoreType.DMA
    vmem, hbm = pl.BlockSpec(memory_space=pltpu.VMEM), pl.BlockSpec(memory_space=pl.ANY)
    n, u, hops = len(JOBS), len(UNITS), FWD + BWD
    shapes = [(job_rows(job), job_cols(job)[1]) for job in JOBS]
    last_shapes = [(2, 2, 32, shape[1]) if i in DUAL else (2, *shape) for i, shape in enumerate(shapes)]
    lasts = [F32 if job[2] else BF16 for job in JOBS]
    return pl.pallas_call(
        kernel,
        out_shape=(pltpu.VMEM((ROWS, D), BF16), pltpu.VMEM((DL, FF), F32)),
        in_specs=[hbm, hbm, hbm, hbm],
        out_specs=(vmem, vmem),
        scratch_shapes=[
            *[pltpu.VMEM((NX, ROWS, w), BF16) for w in WIDTH],
            *[pltpu.VMEM((NX, GROUP, w), BF16) for w in WIDTH],
            pltpu.VMEM((ROWS, D), BF16),
            pltpu.VMEM((D // BLOCK, ROWS), F32),
            pltpu.VMEM((NX, FF, GROUP), BF16),
            pltpu.VMEM((FF, D), BF16),
            pltpu.VMEM((DX, FF), F32),
            pltpu.VMEM((NY * NC, ROWS, D), F32),
            pltpu.VMEM((NY, ROWS, D), F32),
            pltpu.VMEM((NY - 1, ROWS, D), BF16),
            pltpu.VMEM((NY - 1, ROWS, D), BF16),
            *[pltpu.VMEM((2, *shape), BF16) for shape in shapes],
            *[pltpu.VMEM((hops - 2, *shape), BF16) for shape in shapes],
            *[pltpu.VMEM(shape, last) for shape, last in zip(last_shapes, lasts)],
            *[pltpu.VMEM(shape, last) for shape, last in zip(last_shapes, lasts)],
            *[pltpu.VMEM(shape, F32) for shape in shapes],
            *[pltpu.VMEM((16 * len(job[0]), shape[1]), F32) for job, shape in zip(JOBS, shapes)],
            *[pltpu.VMEM((16 * len(job[0]), shape[1]), F32) for job, shape in zip(JOBS, shapes)],
            *[pltpu.VMEM((2, *shapes[i]), F32) for i in DUAL],
            dma((3 + D // WCHUNK,)),
            dma((6,)), dma((6,)), dma((10,)), dma((10,)), dma((10,)), dma((10,)),
            dma((3 * u,)), dma((3 * u,)), dma((4,)), dma((4,)), dma((3,)), dma((3,)),
            dma((hops * n,)), dma((hops * n,)), dma((n,)), dma((n,)),
            dma((2 * len(DUAL),)), dma((2 * len(DUAL),)),
        ],
        compiler_params=pltpu.CompilerParams(
            collective_id=0, has_side_effects=True, vmem_limit_bytes=56 * 2**20
        ),
        cost_estimate=pl.CostEstimate(flops=4 * GROUP * D * FF, bytes_accessed=12 * 2**20, transcendentals=0),
    )(x_saved, block_scales.T, gate_grad.T, gate_weight.T)


def solution(mesh):
    return jax.shard_map(
        shards,
        mesh=mesh,
        in_specs=(
            P(("dp", "tensor"), None),
            P(("dp", "tensor"), None),
            P("dp", "tensor"),
            P(None, "tensor"),
        ),
        out_specs=(P(("dp", "tensor"), None), P("dp", "tensor")),
        check_vma=False,
    )
```

```python
import math

import jax
import jax.numpy as jnp
from jax import lax
from jax.experimental import pallas as pl
from jax.experimental.pallas import tpu as pltpu
from jax.sharding import PartitionSpec as P

MESH = pl.DeviceIdType.MESH
F32, BF16 = jnp.float32, jnp.bfloat16

NX, NZ, NL, NY, NC = 4, 12, 2, 4, 2
D, FF = 2688, 1600
ROWS, GROUP = 32, 256
DX, DL = D // NX, D // (NX * NZ * NL)
BLOCK = 128
PER = (16, 12)
HALF = tuple(NL * p for p in PER)
WIDTH = tuple(NZ * h for h in HALF)
UNITS = ((0, 256), (256, 256), (512, 256), (768, 256), (1024, 256), (1280, 320))
JOBS = (
    ((0,), (0,), True),
    ((0,), (1,), True),
    ((1,), (0, 1), True),
    ((0, 1), (2,), True),
    ((0, 1), (3,), True),
    ((0, 1), (4,), False),
    ((0, 1), (5,), False),
)
DUAL = (5, 6)
ORDER = (
    "pack0", "scatter0", "own0", "pack1", "scatter1", "own1", "ig0", "ig1", "ig2", "ig3", "fwd0", "ig4", "ig5",
    "rest0", "ig6", "igmate", "fwd1", "rest1", "mate01", "mate03", "fwd2", "mate11", "mate13", "fwd3", "mate02",
    "st00", "st10", "mate12", "igo1", "igo2", "igo3", "st20", "st01", "st11", "fwd4", "st30", "st21", "st02", "st12",
    "st40", "st31", "fwd5", "st22", "st03", "st13", "st41", "st32", "st50", "st04", "st14", "st23", "st60", "st42",
    "st33", "st51", "st05", "st15", "st24", "st61", "igfin", "st43", "st34", "close0", "close1", "st52", "st25",
    "st62", "st35", "fin0", "st44", "fin1", "close2", "st53", "st63", "close3", "st45", "fin2", "st54", "st64",
    "fin3", "close4", "st55", "st65", "fin4", "fin5", "fin6",
)
FWD, BWD = 6, 5
WCHUNK = 384


def job_rows(job):
    return sum(HALF[h] for h in job[0])


def job_cols(job):
    first, last = UNITS[job[1][0]], UNITS[job[1][-1]]
    return first[0], last[0] + last[1] - first[0]


def kernel(x_ref, scale_ref, grad_ref, weight_ref, ig_ref, wg_ref, *scratch):
    scratch = list(scratch)

    def take(count=None):
        if count is None:
            return scratch.pop(0)
        return [scratch.pop(0) for _ in range(count)]

    n, h2 = len(JOBS), len(HALF)
    pack, a_buf = take(h2), take(h2)
    x_buf, scale_buf, g_buf, w_buf, part, ig_part, ig_core, ig_send, ig_recv = take(9)
    first_out, slots, last_out, last_in, total_buf, low_out, low_in = (take(n) for _ in range(7))
    value_buf = dict(zip(DUAL, take(len(DUAL))))
    (load_sem, a2a_s, a2a_r, ya_s, ya_r, ca_s, ca_r, g_s, g_r, ic_s, ic_r, iy_s, iy_r,
     z_s, z_r, l_s, l_r, o_s, o_r) = scratch

    dp, tensor = lax.axis_index("dp"), lax.axis_index("tensor")
    x, z, yl = dp // (NZ * NL), (dp // NL) % NZ, dp % NL
    yh, c = tensor // NC, tensor % NC
    s = 1 - 2 * c

    def at(x=x, z=z, yl=yl, yh=yh, c=c):
        return ((x * NZ + z) * NL + yl, yh * NC + c)

    x_to, x_from = (x + s + NX) % NX, (x - s + NX) % NX
    z_to, z_from = (z - s + NZ) % NZ, (z + s + NZ) % NZ
    y_to, y_from, y_opp = (yh + s + NY) % NY, (yh - s + NY) % NY, (yh + 2) % NY
    slot_to, slot_from = (NX + s) % NX, (NX - s) % NX
    mate = at(c=1 - c)
    x_other = [(x + k) % NX for k in range(NX)]
    y_other = [(yh + k) % NY for k in range(NY)]

    pending = []

    def send(src, dst, send_sem, recv_sem, device):
        copy = pltpu.make_async_remote_copy(
            src_ref=src, dst_ref=dst, send_sem=send_sem, recv_sem=recv_sem,
            device_id=device, device_id_type=MESH,
        )
        copy.start()
        pending.append(copy)

    def arrived(dst, sem):
        pltpu.make_async_copy(dst, dst, sem).wait()

    loads = []
    for k, (src, dst) in enumerate(((x_ref, x_buf), (scale_ref, scale_buf))):
        load = pltpu.make_async_copy(src, dst, load_sem.at[1 + D // WCHUNK + k])
        load.start()
        loads.append(load)

    barrier = pltpu.get_barrier_semaphore()
    partners = [at(x=o) for o in x_other[1:]] + [at(yh=o) for o in y_other[1:]] + [
        at(z=z_to), at(z=z_from), at(z=z_to, yl=1 - yl), at(z=z_from, yl=1 - yl), at(yl=1 - yl), mate]
    for partner in partners:
        pl.semaphore_signal(barrier, inc=1, device_id=partner, device_id_type=MESH)

    own_grad = pltpu.make_async_copy(grad_ref, g_buf.at[0], load_sem.at[0])
    own_grad.start()
    weights = []
    for k in range(D // WCHUNK):
        cols = pl.ds(k * WCHUNK, WCHUNK)
        load = pltpu.make_async_copy(weight_ref.at[:, cols], w_buf.at[:, cols], load_sem.at[1 + k])
        load.start()
        weights.append(load)

    for load in loads:
        load.wait()
    scale = scale_buf[...].T
    scaled = jnp.concatenate(
        [(x_buf[:, b * BLOCK:(b + 1) * BLOCK].astype(F32) * scale[:, b:b + 1]).astype(BF16)
         for b in range(D // BLOCK)],
        axis=1,
    ).astype(F32)

    def token_rows(yh, c):
        return pl.ds(pl.multiple_of((yh * NC + c) * ROWS, ROWS), ROWS)

    mine = token_rows(yh, c)

    def pack_half(h):
        for k in range(NX):
            pack[h][k] = jnp.concatenate(
                [scaled[:, k * DX + DL * j + sum(PER[:h]):k * DX + DL * j + sum(PER[:h + 1])]
                 for j in range(NZ * NL)],
                axis=1,
            ).astype(BF16)

    def scatter_half(h):
        for k in range(1, NX):
            index = 3 * h + k - 1
            send(pack[h].at[x_other[k]], a_buf[h].at[NX - k, mine], a2a_s.at[index], a2a_r.at[index],
                 at(x=x_other[k]))
        a_buf[h][0, mine] = pack[h][x]
        share(h, 0)

    def columns(p):
        return pl.ds(0, 1) if p == 0 else pl.ds(1, NX - 1)

    def share(h, p):
        block = a_buf[h].at[columns(p), mine]
        for k, target in enumerate((y_to, y_from)):
            index = h * 5 + k * 2 + p
            send(block, block, ya_s.at[index], ya_r.at[index], at(yh=target))
        send(block, block, ca_s.at[h * 2 + p], ca_r.at[h * 2 + p], mate)

    def share_rest(h):
        for k in range(1, NX):
            index = 3 * h + k - 1
            arrived(a_buf[h].at[NX - k, mine], a2a_r.at[index])
        share(h, 1)

    def to_mate(h, k):
        block = a_buf[h].at[:, token_rows((y_from, y_opp, y_to)[k - 1], c)]
        if k == 2:
            arrived(block, ya_r.at[h * 5 + 4])
        else:
            for p in (0, 1):
                part_ = a_buf[h].at[columns(p), token_rows(y_from if k == 1 else y_to, c)]
                arrived(part_, ya_r.at[h * 5 + (k // 2) * 2 + p])
        if k == 1:
            send(block, block, ya_s.at[h * 5 + 4], ya_r.at[h * 5 + 4], at(yh=y_to))
        index = 4 + h * 3 + k - 1
        send(block, block, ca_s.at[index], ca_r.at[index], mate)

    def inputs_ready(h):
        for p in (0, 1):
            arrived(a_buf[h].at[columns(p), token_rows(yh, 1 - c)], ca_r.at[h * 2 + p])
        for k, source in enumerate((y_to, y_opp, y_from)):
            arrived(a_buf[h].at[:, token_rows(source, 1 - c)], ca_r.at[4 + h * 3 + k])

    def grad_own(i):
        units = pl.ds(*UNITS[i])
        for k, (target, slot) in enumerate(((x_to, slot_from), (x_from, slot_to))):
            send(grad_ref.at[units], g_buf.at[slot, units], g_s.at[3 * i + k], g_r.at[3 * i + k], at(x=target))

    def grad_forward(i):
        units = pl.ds(*UNITS[i])
        arrived(g_buf.at[slot_from, units], g_r.at[3 * i])
        send(g_buf.at[slot_from, units], g_buf.at[2, units], g_s.at[3 * i + 2], g_r.at[3 * i + 2], at(x=x_to))

    def grad_ready(i):
        units = pl.ds(*UNITS[i])
        arrived(g_buf.at[slot_to, units], g_r.at[3 * i + 1])
        arrived(g_buf.at[2, units], g_r.at[3 * i + 2])

    def ig_chunk(k):
        if k == 0:
            own_grad.wait()
        weights[k].wait()
        cols = pl.ds(k * WCHUNK, WCHUNK)
        prod = lax.dot_general(
            g_buf[0], w_buf[:, cols], (((0,), (0,)), ((), ())), preferred_element_type=F32
        )
        ig_part[:, :, cols] = prod.reshape(NY * NC, ROWS, WCHUNK)

    def ig_to_mate():
        for k in range(NY):
            other = y_other[k]
            send(ig_part.at[other * NC + 1 - c], ig_core.at[other], ic_s.at[k], ic_r.at[k], mate)

    def ig_to_owner(k):
        other = y_other[k]
        arrived(ig_core.at[other], ic_r.at[k])
        ig_send[k - 1] = (ig_part[other * NC + c] + ig_core[other]).astype(BF16)
        send(ig_send.at[k - 1], ig_recv.at[k - 1], iy_s.at[k - 1], iy_r.at[k - 1], at(yh=other))

    def ig_finish():
        arrived(ig_core.at[yh], ic_r.at[0])
        total = ig_part[yh * NC + c] + ig_core[yh]
        for k in range(1, NY):
            arrived(ig_recv.at[k - 1], iy_r.at[k - 1])
            total = total + ig_recv[k - 1].astype(F32)
        ig_ref[...] = total.astype(BF16)

    half_seen, unit_seen = set(), set()

    def multiply(i):
        halves, units, _ = JOBS[i]
        for u in units:
            if u not in unit_seen:
                unit_seen.add(u)
                grad_ready(u)
        for h in halves:
            if h not in half_seen:
                half_seen.add(h)
                inputs_ready(h)
        cols = pl.ds(*job_cols(JOBS[i]))
        for h in halves:
            total = None
            for k in range(NX):
                prod = lax.dot_general(
                    a_buf[h][k], g_buf[k, cols], (((0,), (1,)), ((), ())), preferred_element_type=F32
                )
                total = prod if k == 0 else total + prod
            part[sum(WIDTH[:h]):sum(WIDTH[:h + 1]), cols] = total

    def own_part(i, owner):
        cols = pl.ds(*job_cols(JOBS[i]))
        blocks = [
            part[pl.ds(pl.multiple_of(sum(WIDTH[:h]) + owner * HALF[h], 8), HALF[h]), cols] for h in JOBS[i][0]
        ]
        return blocks[0] if len(blocks) == 1 else jnp.concatenate(blocks, axis=0)

    def step(i, j):
        if j == 0:
            multiply(i)
            if i in DUAL:
                total_buf[i][...] = own_part(i, z)
                low_send(i)
        for d, (hops, target, sign) in enumerate(((FWD, z_to, -s), (BWD, z_from, s))):
            if j >= hops:
                continue
            base, sem = d * (FWD - 1), i * (FWD + BWD) + d * FWD
            value = own_part(i, (z + sign * (hops - j) + NZ) % NZ)
            if j > 0:
                arrived(slots[i].at[base + j - 1], z_r.at[sem + j - 1])
                value = value + slots[i][base + j - 1].astype(F32)
            if j == hops - 1 and i in DUAL:
                last_both(i, d, value, target, sem + j)
                continue
            if j == hops - 1:
                last_out[i][d] = value.astype(last_out[i].dtype)
                src, dst = last_out[i].at[d], last_in[i].at[d]
            elif j == 0:
                first_out[i][d] = value.astype(BF16)
                src, dst = first_out[i].at[d], slots[i].at[base]
            else:
                slots[i][base + j - 1] = value.astype(BF16)
                src, dst = slots[i].at[base + j - 1], slots[i].at[base + j]
            send(src, dst, z_s.at[sem + j], z_r.at[sem + j], at(z=target))

    def low_blocks(i, ref, low):
        base, blocks = 0, []
        for h in JOBS[i][0]:
            blocks.append(ref[pl.ds(pl.multiple_of(base + low * (8 * (h == 1) + 16 * (h == 0)), 8), 16), :])
            base += HALF[h]
        return blocks

    def low_send(i):
        for k, block in enumerate(low_blocks(i, total_buf[i], 1 - yl)):
            low_out[i][16 * k:16 * k + 16, :] = block
        send(low_out[i], low_in[i], l_s.at[i], l_r.at[i], at(yl=1 - yl))

    def last_both(i, d, value, target, sem):
        scratch_ = value_buf[i].at[d]
        scratch_[...] = value
        for q, low in enumerate((yl, 1 - yl)):
            for k, block in enumerate(low_blocks(i, scratch_, low)):
                last_out[i][d, q, 16 * k:16 * k + 16, :] = block.astype(BF16)
            index = 2 * DUAL.index(i) + d
            ss, rs = (z_s.at[sem], z_r.at[sem]) if q == 0 else (o_s.at[index], o_r.at[index])
            send(last_out[i].at[d, q], last_in[i].at[d, q], ss, rs, at(z=target, yl=low))

    def close(i):
        arrived(last_in[i].at[0], z_r.at[i * (FWD + BWD) + FWD - 1])
        arrived(last_in[i].at[1], z_r.at[i * (FWD + BWD) + FWD + BWD - 1])
        total_buf[i][...] = own_part(i, z) + last_in[i][0].astype(F32) + last_in[i][1].astype(F32)
        low_send(i)

    def finish(i):
        arrived(low_in[i], l_r.at[i])
        extra = None
        if i in DUAL:
            for d, hops in enumerate((FWD, BWD)):
                arrived(last_in[i].at[d, 0], z_r.at[i * (FWD + BWD) + d * FWD + hops - 1])
                arrived(last_in[i].at[d, 1], o_r.at[2 * DUAL.index(i) + d])
            extra = sum(last_in[i][d, q].astype(F32) for d in (0, 1) for q in (0, 1))
        cols = pl.ds(*job_cols(JOBS[i]))
        for k, (h, block) in enumerate(zip(JOBS[i][0], low_blocks(i, total_buf[i], yl))):
            total = block + low_in[i][16 * k:16 * k + 16, :]
            if extra is not None:
                total = total + extra[16 * k:16 * k + 16]
            total = total * (1.0 / math.sqrt(GROUP * NX * NZ * NL))
            if h == 0:
                wg_ref[0:16, cols] = total
            else:
                wg_ref[16:28, cols] = jnp.where(yl == 0, total[:12], total[4:])

    def enter(h):
        if h == 0:
            pl.semaphore_wait(barrier, len(partners))
        scatter_half(h)

    def forward(i):
        grad_forward(i)
        if i + 2 < len(UNITS):
            grad_own(i + 2)

    what = dict(pack=pack_half, scatter=enter, own=grad_own, rest=share_rest, fwd=forward, mate=to_mate, ig=ig_chunk,
                igmate=ig_to_mate, igo=ig_to_owner, igfin=ig_finish, st=step, close=close, fin=finish)
    for name in ORDER:
        word = name.rstrip("0123456789")
        what[word](*(int(digit) for digit in name[len(word):]))
    for copy in pending:
        copy.wait_send()


def shards(x_saved, block_scales, gate_grad, gate_weight):
    dma = pltpu.SemaphoreType.DMA
    vmem, hbm = pl.BlockSpec(memory_space=pltpu.VMEM), pl.BlockSpec(memory_space=pl.ANY)
    n, u, hops = len(JOBS), len(UNITS), FWD + BWD
    shapes = [(job_rows(job), job_cols(job)[1]) for job in JOBS]
    last_shapes = [(2, 2, 32, shape[1]) if i in DUAL else (2, *shape) for i, shape in enumerate(shapes)]
    lasts = [F32 if job[2] else BF16 for job in JOBS]
    return pl.pallas_call(
        kernel,
        out_shape=(pltpu.VMEM((ROWS, D), BF16), pltpu.VMEM((DL, FF), F32)),
        in_specs=[hbm, hbm, hbm, hbm],
        out_specs=(vmem, vmem),
        scratch_shapes=[
            *[pltpu.VMEM((NX, ROWS, w), BF16) for w in WIDTH],
            *[pltpu.VMEM((NX, GROUP, w), BF16) for w in WIDTH],
            pltpu.VMEM((ROWS, D), BF16),
            pltpu.VMEM((D // BLOCK, ROWS), F32),
            pltpu.VMEM((NX, FF, GROUP), BF16),
            pltpu.VMEM((FF, D), BF16),
            pltpu.VMEM((DX, FF), F32),
            pltpu.VMEM((NY * NC, ROWS, D), F32),
            pltpu.VMEM((NY, ROWS, D), F32),
            pltpu.VMEM((NY - 1, ROWS, D), BF16),
            pltpu.VMEM((NY - 1, ROWS, D), BF16),
            *[pltpu.VMEM((2, *shape), BF16) for shape in shapes],
            *[pltpu.VMEM((hops - 2, *shape), BF16) for shape in shapes],
            *[pltpu.VMEM(shape, last) for shape, last in zip(last_shapes, lasts)],
            *[pltpu.VMEM(shape, last) for shape, last in zip(last_shapes, lasts)],
            *[pltpu.VMEM(shape, F32) for shape in shapes],
            *[pltpu.VMEM((16 * len(job[0]), shape[1]), F32) for job, shape in zip(JOBS, shapes)],
            *[pltpu.VMEM((16 * len(job[0]), shape[1]), F32) for job, shape in zip(JOBS, shapes)],
            *[pltpu.VMEM((2, *shapes[i]), F32) for i in DUAL],
            dma((3 + D // WCHUNK,)),
            dma((6,)), dma((6,)), dma((10,)), dma((10,)), dma((10,)), dma((10,)),
            dma((3 * u,)), dma((3 * u,)), dma((4,)), dma((4,)), dma((3,)), dma((3,)),
            dma((hops * n,)), dma((hops * n,)), dma((n,)), dma((n,)),
            dma((2 * len(DUAL),)), dma((2 * len(DUAL),)),
        ],
        compiler_params=pltpu.CompilerParams(
            collective_id=0, has_side_effects=True, vmem_limit_bytes=56 * 2**20
        ),
        cost_estimate=pl.CostEstimate(flops=4 * GROUP * D * FF, bytes_accessed=12 * 2**20, transcendentals=0),
    )(x_saved, block_scales.T, gate_grad.T, gate_weight.T)


def solution(mesh):
    return jax.shard_map(
        shards,
        mesh=mesh,
        in_specs=(
            P(("dp", "tensor"), None),
            P(("dp", "tensor"), None),
            P("dp", "tensor"),
            P(None, "tensor"),
        ),
        out_specs=(P(("dp", "tensor"), None), P("dp", "tensor")),
        check_vma=False,
    )
```
